1024 devices in a mesh: row: 16 (over z, core), col: 64 (over y, x).
Axes of the slice: x: 8, y: 8, z: 8, core: 2. Of those that a mesh axis runs over, the one named last changes fastest.
Arguments:
- features: float32 [131072, 128], P(('col', 'row')), may hold values from -6 to 6
- weight: float32 [128, 128], replicated, may hold values from -0.5 to 0.5
- adj_tiles: float32 [16, 64, 32, 128, 128], P('row', 'col'), may hold values from -0.0625 to 0.0625
- tile_row: int32 [16, 64, 32], P('row', 'col'), may hold values from 0 to 63
- tile_col: int32 [16, 64, 32], P('row', 'col'), may hold values from 0 to 15
- slot_count: int32 [16, 64], P('row', 'col'), may hold values from 4 to 32, as said below
- cotangent: float32 [131072, 128], P(('row', 'col')), may hold values from -6 to 6
Outputs:
- hidden: float32 [131072, 128], P(('row', 'col'))
- grad_input: float32 [131072, 128], P(('col', 'row'))
- grad_weight: float32 [128, 128], replicated
The draws below stay inside these ranges and needn't reach their ends.
Inputs may be any that keep to these rules, and one draw needn't show every extreme that they name: `slot_count`: some device has all 32 slots live; the others have 32 divided by 1, 2, 4 or 8.
All inputs are finite; a program needn't handle non-finite values.
Results may differ from the reference program's by a relative error of at most 0.0003.
Values sent between devices are 32-bit elements; how exact they have to be, the bound alone decides.
A program may use at most 64 MiB of HBM per device.

```python
import math
import jax
import jax.numpy as jnp
import numpy as np
from jax import lax

F = 128
TILE = 128
TILES_DEV = 32
NODES = 131072
R_TILES = 64
C_TILES = 16
N_ROW = 16
N_COL = 64


def draw_slot_count(key, part):
    key = jax.random.fold_in(key, 7)
    first, second = jax.random.split(key)
    shifts = jax.random.randint(first, (N_ROW * N_COL,), 0, 4)
    counts = jnp.maximum(TILES_DEV // jnp.left_shift(jnp.ones_like(shifts), shifts), 1)
    chosen = jax.random.randint(second, (), 0, N_ROW * N_COL)
    counts = jnp.where(jnp.arange(N_ROW * N_COL) == chosen, TILES_DEV, counts)
    return counts.reshape(N_ROW, N_COL).astype(jnp.int32)


def with_ends(result, own_key, low, top_value):
    extent = result.shape
    spot = [jax.random.randint(jax.random.fold_in(own_key, axis), (), 0, extent[axis]) for axis in range(len(extent))]
    result = result.at[tuple(spot)].set(low)
    longest = extent.index(max(extent))
    spot[longest] = (spot[longest] + 1) % extent[longest]
    return result.at[tuple(spot)].set(top_value)


def steps_of(stream_key, shape, pieces, low, top_value):
    gain = 1.0
    for dim, blocks in pieces:
        heights = jax.random.uniform(jax.random.fold_in(jax.random.fold_in(stream_key, 6), dim), (blocks,), jnp.float32, low / len(pieces), top_value / len(pieces))
        gain = gain * jnp.repeat(jnp.exp(heights), shape[dim] // blocks).reshape((-1,) + (1,) * (len(shape) - 1 - dim))
    return gain


def rank_table(number_of, skew):
    portions = [(1 << 20) // math.isqrt(rank ** skew) + 1 for rank in range(1, number_of + 1)]
    spread = 1 + sum(portions) // (1 << 30)
    return np.cumsum(np.array([max(1, weight // spread) for weight in portions]))


def ranked(stream_key, shape, number_of, skew):
    listing = rank_table(number_of, skew)
    ticket = jax.random.randint(jax.random.fold_in(stream_key, 1), shape, 0, int(listing[number_of - 1]))
    rank = jnp.searchsorted(jnp.asarray(listing, jnp.int32), ticket, side="right")
    return jax.random.permutation(jax.random.fold_in(stream_key, 2), number_of)[rank].astype(jnp.int32)


def noise(key, shape, deviation, limit, cuts=(), held_as=jnp.bfloat16):
    gain = steps_of(key, shape, cuts, -0.22, 0.18) if cuts else 1.0
    array = jax.random.normal(key, shape, jnp.float32) * deviation * gain
    return jnp.minimum(jnp.maximum(array, -limit), limit).astype(held_as)


def setup_inputs(seed: int = 0) -> dict:
    arg_keys = jax.random.split(jax.random.key(seed), 8)
    return {
        "features": noise(arg_keys[0], (NODES, F), 1.0, 6.0, ((0, 1024),), jnp.float32),
        "weight": noise(arg_keys[1], (F, F), F ** -0.5, 0.5, (), jnp.float32),
        "adj_tiles": noise(arg_keys[2], (N_ROW, N_COL, TILES_DEV, TILE, TILE), (2.0 / (TILES_DEV * N_COL * TILE) ** 0.5), 0.0625, ((0, 16), (1, 64)), jnp.float32),
        "tile_row": with_ends(ranked(arg_keys[3], (N_ROW, N_COL, TILES_DEV), R_TILES, 2), jax.random.fold_in(arg_keys[3], 3), 0, R_TILES - 1).astype(jnp.int32),
        "tile_col": with_ends(jax.random.randint(arg_keys[4], (N_ROW, N_COL, TILES_DEV), 0, C_TILES), jax.random.fold_in(arg_keys[4], 1), 0, C_TILES - 1).astype(jnp.int32),
        "slot_count": draw_slot_count(jax.random.fold_in(arg_keys[7], 71), 0),
        "cotangent": noise(arg_keys[6], (NODES, F), 1.0, 6.0, ((0, 1024),), jnp.float32),
    }


def gelu_tanh(values):
    return jax.nn.gelu(values, approximate=True)

def reference(features, weight, adj_tiles, tile_row, tile_col, slot_count, cotangent):
    highest = lax.Precision.HIGHEST
    devices = N_ROW * N_COL
    projected = jnp.dot(features, weight, precision=highest, preferred_element_type=jnp.float32)
    proj_blocks = projected.reshape(N_COL, C_TILES, TILE, F)
    flat_tiles = adj_tiles.reshape(devices, TILES_DEV, TILE, TILE)
    flat_rows = tile_row.reshape(devices, TILES_DEV)
    flat_cols = tile_col.reshape(devices, TILES_DEV)
    flat_count = slot_count.reshape(devices)
    slot_ids = jnp.arange(TILES_DEV, dtype=jnp.int32)
    device_ids = jnp.arange(devices, dtype=jnp.int32)

    def forward_step(total, inputs):
        block, rows, cols, count, device = inputs
        grid_row = device // N_COL
        grid_col = device % N_COL
        source = proj_blocks[grid_col]
        picked = source[cols]
        product = jnp.einsum('tij,tjf->tif', block, picked, precision=highest)
        product = jnp.where((slot_ids < count)[:, None, None], product, jnp.float32(0.0))
        partial_value = jax.ops.segment_sum(product, rows, num_segments=R_TILES)
        return (total.at[grid_row].add(partial_value), None)
    start_total = jnp.zeros((N_ROW, R_TILES, TILE, F), jnp.float32)
    aggregate, _ = lax.scan(forward_step, start_total, (flat_tiles, flat_rows, flat_cols, flat_count, device_ids))
    aggregate = aggregate.reshape(NODES, F)
    hidden, grad_fn = jax.vjp(gelu_tanh, aggregate)
    grad_pre = grad_fn(cotangent)[0]
    pre_blocks = grad_pre.reshape(N_ROW, R_TILES, TILE, F)

    def backward_step(total, inputs):
        block, rows, cols, count, device = inputs
        grid_row = device // N_COL
        grid_col = device % N_COL
        source = pre_blocks[grid_row]
        picked = source[rows]
        product = jnp.einsum('tji,tjf->tif', block, picked, precision=highest)
        product = jnp.where((slot_ids < count)[:, None, None], product, jnp.float32(0.0))
        partial_value = jax.ops.segment_sum(product, cols, num_segments=C_TILES)
        return (total.at[grid_col].add(partial_value), None)
    start_grad = jnp.zeros((N_COL, C_TILES, TILE, F), jnp.float32)
    grad_projected, _ = lax.scan(backward_step, start_grad, (flat_tiles, flat_rows, flat_cols, flat_count, device_ids))
    grad_projected = grad_projected.reshape(NODES, F)
    grad_input = jnp.dot(grad_projected, weight.T, precision=highest, preferred_element_type=jnp.float32)
    grad_weight = jnp.dot(features.T, grad_projected, precision=highest, preferred_element_type=jnp.float32)
    return (hidden, grad_input, grad_weight)
```

```python
import functools
import jax
import jax.numpy as jnp
from jax import lax
from jax.experimental import pallas as pl
from jax.experimental.pallas import tpu as pltpu
from jax.sharding import PartitionSpec as P

MESH = pl.DeviceIdType.MESH
T = 128
NX = 8
F32 = jnp.float32
BF16 = jnp.bfloat16
VMEM = pl.BlockSpec(memory_space=pltpu.VMEM)
SMEM = pl.BlockSpec(memory_space=pltpu.SMEM)
LIMIT = 40 * 1024 * 1024


def split(value):
    high = value.astype(BF16)
    low = (value - high.astype(F32)).astype(BF16)
    return high, low


def dot3(left, right):
    lh, ll = split(left)
    rh, rl = split(right)
    return jnp.dot(
        jnp.concatenate([lh, ll, lh], axis=1),
        jnp.concatenate([rh, rh, rl], axis=0),
        preferred_element_type=F32,
    )


def steps_of(n, sign, half):
    return n // 2 if (sign > 0) == (half == 0) else n // 2 - 1


CHAINS = ((1, 0), (-1, 1), (1, 1), (-1, 0))


def wrap(index, n):
    return lax.rem(index + n, n)


def greet(peers):
    barrier = pltpu.get_barrier_semaphore()
    total = 0
    for count, device in peers:
        def one(k, carry, device=device):
            pl.semaphore_signal(barrier, inc=1, device_id=device(k), device_id_type=MESH)
            return carry
        lax.fori_loop(1, count + 1, one, 0)
        total += count
    pl.semaphore_wait(barrier, total)


def remote(src, dst, send, recv, device):
    return pltpu.make_async_remote_copy(
        src_ref=src, dst_ref=dst, send_sem=send, recv_sem=recv, device_id=device, device_id_type=MESH
    )


def z_gather_kernel(nz, x_ref, out_ref, ring_send, ring_recv, pair_send, pair_recv):
    row, col = lax.axis_index("row"), lax.axis_index("col")
    z, c = row // 2, lax.rem(row, 2)
    half_rows = T // 2
    ring = {s: (wrap(z + s, nz) * 2 + c, col) for s in (1, -1)}
    pair = (z * 2 + 1 - c, col)
    greet([(1, lambda k: ring[1]), (1, lambda k: ring[-1]), (1, lambda k: pair)])
    out_ref[z, c] = x_ref[...]

    def piece(zz, cc, half):
        return out_ref.at[zz, cc, pl.ds(half * half_rows, half_rows), :]

    def hop(i, t):
        sign, half = CHAINS[i]
        zz = wrap(z - sign * t, nz)
        return remote(piece(zz, c, half), piece(zz, c, half), ring_send.at[i, t], ring_recv.at[i, t], ring[sign])

    def arrival(i, t):
        sign, half = CHAINS[i]
        zz = wrap(z - sign * (t + 1), nz)
        return remote(piece(zz, c, half), piece(zz, c, half), ring_send.at[i, t], ring_recv.at[i, t], ring[sign])

    def share(i, t, cc):
        sign, half = CHAINS[i]
        zz = wrap(z - sign * (t + 1), nz)
        return remote(piece(zz, cc, half), piece(zz, cc, half), pair_send.at[i, t], pair_recv.at[i, t], pair)

    def own(cc):
        return remote(out_ref.at[z, cc], out_ref.at[z, cc], pair_send.at[4, 0], pair_recv.at[4, 0], pair)

    deep = [steps_of(nz, *chain) for chain in CHAINS]
    for i in range(4):
        hop(i, 0).start()
    own(c).start()
    for t in range(nz // 2):
        for i in range(4):
            if t < deep[i]:
                arrival(i, t).wait_recv()
                if t + 1 < deep[i]:
                    hop(i, t + 1).start()
                share(i, t, c).start()
    own(1 - c).wait_recv()
    for t in range(nz // 2):
        for i in range(4):
            if t < deep[i]:
                share(i, t, 1 - c).wait_recv()
    own(c).wait_send()
    for t in range(nz // 2):
        for i in range(4):
            if t < deep[i]:
                hop(i, t).wait_send()
                share(i, t, c).wait_send()


def z_gather(features, nz):
    return pl.pallas_call(
        functools.partial(z_gather_kernel, nz),
        out_shape=jax.ShapeDtypeStruct((nz, 2, T, T), F32),
        in_specs=[VMEM],
        out_specs=VMEM,
        scratch_shapes=[
            pltpu.SemaphoreType.DMA((4, nz // 2)),
            pltpu.SemaphoreType.DMA((4, nz // 2)),
            pltpu.SemaphoreType.DMA((5, nz // 2)),
            pltpu.SemaphoreType.DMA((5, nz // 2)),
        ],
        compiler_params=pltpu.CompilerParams(collective_id=0, has_side_effects=True, vmem_limit_bytes=LIMIT),
        name="z_gather",
    )(features)


GROUP = 4


def forward_kernel(rows, cols, count, adj, x, out, triple):
    out[...] = jnp.zeros_like(out)

    def prepare(c, carry):
        high, low = split(x[c])
        triple[c] = jnp.concatenate([high, high, low], axis=0)
        return carry

    lax.fori_loop(0, x.shape[0], prepare, 0)

    def group(g, carry):
        products = []
        for u in range(GROUP):
            s = g * GROUP + u
            high, low = split(adj[s])
            left = jnp.concatenate([high, low, high], axis=1)
            products.append(jnp.dot(left, triple[cols[s]], preferred_element_type=F32))
        for u in range(GROUP):
            r = rows[g * GROUP + u]
            out[r] = out[r] + products[u]
        return carry

    lax.fori_loop(0, count[0] // GROUP, group, 0)


def forward(rows, cols, count, adj, x, row_tiles):
    return pl.pallas_call(
        forward_kernel,
        out_shape=jax.ShapeDtypeStruct((row_tiles, T, T), F32),
        in_specs=[SMEM, SMEM, SMEM, VMEM, VMEM],
        out_specs=VMEM,
        scratch_shapes=[pltpu.VMEM((x.shape[0], 3 * T, T), BF16)],
        compiler_params=pltpu.CompilerParams(vmem_limit_bytes=LIMIT),
        name="forward_tiles",
    )(rows, cols, count, adj, x)


def backward_kernel(rows, cols, count, adj, g, out):
    out[...] = jnp.zeros_like(out)

    def group(i, carry):
        products = []
        for u in range(GROUP):
            s = i * GROUP + u
            products.append(dot3(g[rows[s]], adj[s]))
        for u in range(GROUP):
            c = cols[i * GROUP + u]
            out[c] = out[c] + products[u]
        return carry

    lax.fori_loop(0, count[0] // GROUP, group, 0)


def backward(rows, cols, count, adj, g, col_tiles):
    return pl.pallas_call(
        backward_kernel,
        out_shape=jax.ShapeDtypeStruct((col_tiles, T, T), F32),
        in_specs=[SMEM, SMEM, SMEM, VMEM, VMEM],
        out_specs=VMEM,
        compiler_params=pltpu.CompilerParams(vmem_limit_bytes=LIMIT),
        name="backward_tiles",
    )(rows, cols, count, adj, g)


def xy_kernel(
    ny, nx, nrow, partial, weight, cotangent, hidden, out, grad_weight,
    block, reduced, landed, send1, recv1, send2, recv2, sendA, recvA, sendB, recvB, sendC, recvC,
    lw, part_a, part_b, part_c, sendR, recvR, sendW, recvW,
):
    row, col = lax.axis_index("row"), lax.axis_index("col")
    y, x = col // nx, lax.rem(col, nx)
    size = (nx, ny)
    place = (x, y)
    quarter, half_rows = T // 4, T // 2
    wrows = T // nx

    def at_x(k):
        return (row, y * nx + wrap(x + k, nx))

    def at_y(k):
        return (row, wrap(y + k, ny) * nx + x)

    def at_row(k):
        return (lax.rem(row + k, nrow), col)

    along = (at_x, at_y)
    greet([(nx - 1, at_x), (ny - 1, at_y), (nrow - 1, at_row)])

    def tiles(ref, axis, where, start, count):
        if axis == 0:
            return ref.at[:, where, pl.ds(start, count), :]
        return ref.at[where, :, pl.ds(start, count), :]

    def first_row(axis, half):
        return axis * half_rows + half * quarter

    chains = [(axis, sign, half) for sign, half in CHAINS for axis in (0, 1)]
    deep = [steps_of(size[axis], sign, half) for axis, sign, half in chains]
    most = max(deep)

    def move(i, t):
        axis, sign, half = chains[i]
        if t == 0:
            src = tiles(partial, axis, wrap(place[axis] + sign * deep[i], size[axis]), first_row(axis, half), quarter)
        else:
            src = block.at[i, t - 1]
        return remote(src, block.at[i, t], send1.at[i, t], recv1.at[i, t], along[axis](sign))

    for i in range(len(chains)):
        move(i, 0).start()
    for t in range(1, most + 1):
        for i, (axis, sign, half) in enumerate(chains):
            if t < deep[i]:
                move(i, t - 1).wait_recv()
                mine = tiles(partial, axis, wrap(place[axis] + sign * (deep[i] - t), size[axis]), first_row(axis, half), quarter)
                block[i, t - 1] = block[i, t - 1] + mine[...]
                move(i, t).start()
    for half in (0, 1):
        for axis in (0, 1):
            plus, minus = chains.index((axis, 1, half)), chains.index((axis, -1, half))
            move(plus, deep[plus] - 1).wait_recv()
            move(minus, deep[minus] - 1).wait_recv()
            mine = tiles(partial, axis, place[axis], first_row(axis, half), quarter)
            reduced[axis, :, pl.ds(half * quarter, quarter), :] = (
                mine[...] + block[plus, deep[plus] - 1] + block[minus, deep[minus] - 1]
            )

    def part(axis, k):
        other = 1 - axis
        src = reduced.at[axis, wrap(place[other] + k, size[other])]
        return remote(src, landed.at[axis, place[other]], send2.at[axis, k], recv2.at[axis, k], along[other](k))

    def part_in(axis, k):
        other = 1 - axis
        slot = landed.at[axis, wrap(place[other] - k, size[other])]
        return remote(slot, slot, send2.at[axis, k], recv2.at[axis, k], along[other](-k))

    def loop(first, last, body):
        def step(k, carry):
            body(k)
            return carry
        lax.fori_loop(first, last, step, 0)

    for axis in (0, 1):
        loop(1, size[1 - axis], lambda k: part(axis, k).start())
    for axis in (0, 1):
        landed[axis, place[1 - axis]] = reduced[axis, place[1 - axis]]
    sums = []
    for axis in (0, 1):
        loop(1, size[1 - axis], lambda k: part_in(axis, k).wait_recv())
        total = landed[axis, 0]
        for k in range(1, size[1 - axis]):
            total = total + landed[axis, k]
        sums.append(total)
    summed = jnp.concatenate(sums, axis=0)

    value = dot3(summed, weight[...])
    scale = 0.7978845608028654
    t = jnp.tanh(scale * (value + 0.044715 * value * value * value))
    hidden[...] = 0.5 * value * (1.0 + t)
    slope = 0.5 * (1.0 + t) + 0.5 * value * (1.0 - t * t) * scale * (1.0 + 3.0 * 0.044715 * value * value)
    pre = cotangent[...] * slope
    out[y, x] = dot3(weight[...], pre.T)

    def spread(axis, k):
        other = 1 - axis
        ref = out.at[y, x, pl.ds(axis * half_rows, half_rows), :]
        return remote(ref, ref, sendA.at[axis, k], recvA.at[axis, k], along[other](k))

    def spread_in(axis, k):
        other = 1 - axis
        at = wrap(place[other] - k, size[other])
        ref = (out.at[at, x] if other == 1 else out.at[y, at]).at[pl.ds(axis * half_rows, half_rows), :]
        return remote(ref, ref, sendA.at[axis, k], recvA.at[axis, k], along[other](-k))

    def pass_on(axis, d, k):
        other = 1 - axis
        at = wrap(place[other] - k, size[other])
        ref = (out.at[at, x] if other == 1 else out.at[y, at]).at[pl.ds(axis * half_rows, half_rows), :]
        return remote(ref, ref, sendB.at[axis, d], recvB.at[axis, d], along[axis](1 - 2 * d))

    def passed(axis, d, sent):
        sign = 1 - 2 * d
        at = place[axis] if sent else wrap(place[axis] - sign, size[axis])
        ref = tiles(out, axis, at, axis * half_rows, half_rows)
        return remote(ref, ref, sendB.at[axis, d], recvB.at[axis, d], along[axis](sign))

    for axis in (0, 1):
        loop(1, size[1 - axis], lambda k: spread(axis, k).start())
        for d in (0, 1):
            pass_on(axis, d, 0).start()

    lw[...] = dot3(summed.T, pre)

    def weight_rows(k):
        return pl.ds(k * wrows, wrows)

    def scatter(k):
        at = wrap(x + k, nx)
        return remote(lw.at[weight_rows(at), :], part_a.at[x], sendR.at[0, k], recvR.at[0, k], at_x(k))

    def scatter_in(k):
        slot = part_a.at[wrap(x - k, nx)]
        return remote(slot, slot, sendR.at[0, k], recvR.at[0, k], at_x(-k))

    loop(1, nx, lambda k: scatter(k).start())
    part_a[x] = lw[weight_rows(x), :]

    def forward_tile(k):
        for axis in (0, 1):
            spread_in(axis, k).wait_recv()
            for d in (0, 1):
                pass_on(axis, d, k).start()

    loop(1, nx, forward_tile)

    def swap_y(k):
        return remote(part_b.at[y], part_b.at[y], sendR.at[1, k], recvR.at[1, k], at_y(k))

    def swap_y_in(k):
        slot = part_b.at[wrap(y - k, ny)]
        return remote(slot, slot, sendR.at[1, k], recvR.at[1, k], at_y(-k))

    def swap_row(k):
        return remote(part_c.at[row], part_c.at[row], sendW.at[k], recvW.at[k], at_row(k))

    def swap_row_in(k):
        slot = part_c.at[wrap(row - k, nrow)]
        return remote(slot, slot, sendW.at[k], recvW.at[k], at_row(nrow - k))

    def final(k):
        ref = grad_weight.at[weight_rows(x), :]
        return remote(ref, ref, sendR.at[2, k], recvR.at[2, k], at_x(k))

    def final_in(k):
        ref = grad_weight.at[weight_rows(wrap(x - k, nx)), :]
        return remote(ref, ref, sendR.at[2, k], recvR.at[2, k], at_x(-k))

    def add_up(slots, n):
        total = slots[0]
        for k in range(1, n):
            total = total + slots[k]
        return total

    def reduce_x():
        loop(1, nx, lambda k: scatter_in(k).wait_recv())
        part_b[y] = add_up(part_a, nx)
        loop(1, ny, lambda k: swap_y(k).start())

    def reduce_y():
        loop(1, ny, lambda k: swap_y_in(k).wait_recv())
        part_c[row] = add_up(part_b, ny)
        loop(1, nrow, lambda k: swap_row(k).start())

    def reduce_row():
        loop(1, nrow, lambda k: swap_row_in(k).wait_recv())
        grad_weight[weight_rows(x), :] = add_up(part_c, nrow)
        loop(1, nx, lambda k: final(k).start())

    between = {2: reduce_x, 3: reduce_y, 4: reduce_row}

    def relay(i, t, incoming):
        axis, sign, half = chains[i]
        at = wrap(place[axis] - sign * (t if incoming else t - 1), size[axis])
        ref = tiles(out, axis, at, first_row(axis, half), quarter)
        return remote(ref, ref, sendC.at[i, t], recvC.at[i, t], along[axis](sign))

    for t in range(2, most + 1):
        for i, (axis, sign, half) in enumerate(chains):
            if t == 2 and i in (0, 1, 2, 3):
                passed(axis, (1 - sign) // 2, False).wait_recv()
            if t <= deep[i]:
                if t > 2:
                    relay(i, t - 1, True).wait_recv()
                relay(i, t, False).start()
        between[t]()
    for i in range(len(chains)):
        relay(i, deep[i], True).wait_recv()
    loop(1, nx, lambda k: final_in(k).wait_recv())

    for i in range(len(chains)):
        for t in range(deep[i]):
            move(i, t).wait_send()
        for t in range(2, deep[i] + 1):
            relay(i, t, False).wait_send()
    for axis in (0, 1):
        loop(1, size[1 - axis], lambda k: part(axis, k).wait_send())
        loop(1, size[1 - axis], lambda k: spread(axis, k).wait_send())
        for d in (0, 1):
            passed(axis, d, True).wait_send()
    loop(1, nx, lambda k: scatter(k).wait_send())
    loop(1, ny, lambda k: swap_y(k).wait_send())
    loop(1, nrow, lambda k: swap_row(k).wait_send())
    loop(1, nx, lambda k: final(k).wait_send())


def xy(partial, weight, cotangent, ny, nx, nrow):
    partial = partial.reshape(ny, nx, T, T)
    most = max(nx, ny) // 2
    sem = pltpu.SemaphoreType.DMA
    big = max(nx, ny)
    return pl.pallas_call(
        functools.partial(xy_kernel, ny, nx, nrow),
        out_shape=(
            jax.ShapeDtypeStruct((T, T), F32),
            jax.ShapeDtypeStruct((ny, nx, T, T), F32),
            jax.ShapeDtypeStruct((T, T), F32),
        ),
        in_specs=[VMEM] * 3,
        out_specs=(VMEM,) * 3,
        scratch_shapes=[
            pltpu.VMEM((8, most, big, T // 4, T), F32),
            pltpu.VMEM((2, big, T // 2, T), F32),
            pltpu.VMEM((2, big, T // 2, T), F32),
            sem((8, most)), sem((8, most)),
            sem((2, big)), sem((2, big)),
            sem((2, big)), sem((2, big)),
            sem((2, 2)), sem((2, 2)),
            sem((8, most + 1)), sem((8, most + 1)),
            pltpu.VMEM((T, T), F32),
            pltpu.VMEM((nx, T // nx, T), F32),
            pltpu.VMEM((ny, T // nx, T), F32),
            pltpu.VMEM((nrow, T // nx, T), F32),
            sem((3, big)), sem((3, big)),
            sem((nrow,)), sem((nrow,)),
        ],
        compiler_params=pltpu.CompilerParams(collective_id=1, has_side_effects=True, vmem_limit_bytes=LIMIT),
        name="xy_exchange",
    )(partial, weight, cotangent)


def z_scatter_kernel(nz, part, out, other, block, pair_send, pair_recv, ring_send, ring_recv):
    row, col = lax.axis_index("row"), lax.axis_index("col")
    z, c = row // 2, lax.rem(row, 2)
    half_rows = T // 2
    ring = {s: (wrap(z + s, nz) * 2 + c, col) for s in (1, -1)}
    pair = (z * 2 + 1 - c, col)
    greet([(1, lambda k: ring[1]), (1, lambda k: ring[-1]), (1, lambda k: pair)])

    def give(off):
        zz = wrap(z + off, nz)
        return remote(part.at[zz, 1 - c], other.at[zz], pair_send.at[off % nz], pair_recv.at[off % nz], pair)

    far = nz // 2
    order = [far] + [s * k for k in range(far - 1, 0, -1) for s in (1, -1)] + [0]
    for off in order:
        give(off).start()
    taken = set()

    def take(off):
        if off % nz not in taken:
            taken.add(off % nz)
            give(off).wait_recv()

    def term(off, half):
        take(off)
        zz = wrap(z + off, nz)
        here = pl.ds(half * half_rows, half_rows)
        return part[zz, c, here, :] + other[zz, here, :]

    deep = [steps_of(nz, *chain) for chain in CHAINS]

    def move(i, t):
        return remote(block.at[i, t], block.at[i, t + 1], ring_send.at[i, t], ring_recv.at[i, t], ring[CHAINS[i][0]])

    for t in range(nz // 2):
        for i, (sign, half) in enumerate(CHAINS):
            if t < deep[i]:
                value = term(sign * (deep[i] - t), half)
                if t > 0:
                    move(i, t - 1).wait_recv()
                    value = value + block[i, t]
                block[i, t] = value
                move(i, t).start()
    rows = []
    for half in (0, 1):
        value = term(0, half)
        for i, chain in enumerate(CHAINS):
            if chain[1] == half:
                move(i, deep[i] - 1).wait_recv()
                value = value + block[i, deep[i]]
        rows.append(value)
    out[...] = jnp.concatenate(rows, axis=0).T
    for off in order:
        give(off).wait_send()
    for i in range(4):
        for t in range(deep[i]):
            move(i, t).wait_send()


def z_scatter(part, nz):
    sem = pltpu.SemaphoreType.DMA
    return pl.pallas_call(
        functools.partial(z_scatter_kernel, nz),
        out_shape=jax.ShapeDtypeStruct((T, T), F32),
        in_specs=[VMEM],
        out_specs=VMEM,
        scratch_shapes=[
            pltpu.VMEM((nz, T, T), F32),
            pltpu.VMEM((4, nz // 2 + 1, T // 2, T), F32),
            sem((nz,)), sem((nz,)),
            sem((4, nz // 2)), sem((4, nz // 2)),
        ],
        compiler_params=pltpu.CompilerParams(collective_id=2, has_side_effects=True, vmem_limit_bytes=LIMIT),
        name="z_scatter",
    )(part.reshape(nz, 2, T, T))


def local(nrow, ncol, features, weight, adj_tiles, tile_row, tile_col, slot_count, cotangent):
    nz, nx = nrow // 2, NX
    ny = ncol // nx
    rows, cols, count, adj = tile_row[0, 0], tile_col[0, 0], slot_count[0], adj_tiles[0, 0]
    x = z_gather(features, nz).reshape(nrow, T, T)
    partial = forward(rows, cols, count, adj, x, ncol)
    hidden, pre_rows, grad_weight = xy(partial, weight, cotangent, ny, nx, nrow)
    part = backward(rows, cols, count, adj, pre_rows.reshape(ncol, T, T), nrow)
    return hidden, z_scatter(part, nz), grad_weight


def solution(mesh):
    placed = (
        P(("col", "row"), None),
        P(),
        P("row", "col", None, None, None),
        P("row", "col", None),
        P("row", "col", None),
        P("row", "col"),
        P(("row", "col"), None),
    )
    return jax.shard_map(
        functools.partial(local, mesh.shape["row"], mesh.shape["col"]),
        mesh=mesh,
        in_specs=placed,
        out_specs=(P(("row", "col"), None), P(("col", "row"), None), P()),
        check_vma=False,
    )
```

```python
import functools
import jax
import jax.numpy as jnp
from jax import lax
from jax.experimental import pallas as pl
from jax.experimental.pallas import tpu as pltpu
from jax.sharding import PartitionSpec as P

MESH = pl.DeviceIdType.MESH
T = 128
NX = 8
F32 = jnp.float32
BF16 = jnp.bfloat16
VMEM = pl.BlockSpec(memory_space=pltpu.VMEM)
SMEM = pl.BlockSpec(memory_space=pltpu.SMEM)
HBM = pl.BlockSpec(memory_space=pltpu.HBM)
MIB = 1024 * 1024


def split(value):
    high = value.astype(BF16)
    low = (value - high.astype(F32)).astype(BF16)
    return high, low


def dot3(left, right):
    lh, ll = split(left)
    rh, rl = split(right)
    return jnp.dot(
        jnp.concatenate([lh, ll, lh], axis=1),
        jnp.concatenate([rh, rh, rl], axis=0),
        preferred_element_type=F32,
    )


def wrap(index, n):
    return lax.rem(index + n, n)


def greet(peers):
    barrier = pltpu.get_barrier_semaphore()
    total = 0
    for count, device in peers:
        def one(k, carry, device=device):
            pl.semaphore_signal(barrier, inc=1, device_id=device(k), device_id_type=MESH)
            return carry
        lax.fori_loop(1, count + 1, one, 0)
        total += count
    pl.semaphore_wait(barrier, total)


def remote(src, dst, send, recv, device):
    return pltpu.make_async_remote_copy(
        src_ref=src, dst_ref=dst, send_sem=send, recv_sem=recv, device_id=device, device_id_type=MESH
    )


SIGNS = (1, -1)


def ring_peers(z, c, col, nz):
    return {k: (wrap(z + k, nz) * 2 + c, col) for k in (1, -1, 2, -2)}


def z_gather_kernel(
    nz, x_ref, adj, rows, cols, out_ref, adj_out, rows_out, cols_out,
    send, recv, relay_send, relay_recv, pair_send, pair_recv, fetch_sem,
):
    row, col = lax.axis_index("row"), lax.axis_index("col")
    z, c = row // 2, lax.rem(row, 2)
    half_rows = T // 2
    ring = ring_peers(z, c, col, nz)
    pair = (z * 2 + 1 - c, col)
    own = pltpu.make_async_copy(x_ref, out_ref.at[z, c], fetch_sem.at[0])
    own.start()
    fetches = [
        pltpu.make_async_copy(src, dst, fetch_sem.at[i])
        for i, (src, dst) in enumerate(((adj, adj_out), (rows, rows_out), (cols, cols_out)), 1)
    ]
    greet([(1, lambda k, to=to: to) for to in (*ring.values(), pair)])
    own.wait()

    def piece(off, cc, half):
        ref = out_ref.at[wrap(z + off, nz), cc]
        return ref if half is None else ref.at[pl.ds(half * half_rows, half_rows), :]

    def copy(ref, sems, i, j, to):
        return remote(ref, ref, sems[0].at[i, j], sems[1].at[i, j], to)

    first, second, shared = (send, recv), (relay_send, relay_recv), (pair_send, pair_recv)

    def far(d, half, off):
        return copy(piece(off, c, half), first, d, half, ring[2 * SIGNS[d]])

    def near(d, off):
        return copy(piece(off, c, None), first, d, 2, ring[SIGNS[d]])

    def third(d, half, off):
        return copy(piece(off, c, half), second, d, half, ring[SIGNS[d]])

    def fourth(d, off):
        return copy(piece(off, c, d), second, d, 2, ring[2 * SIGNS[d]])

    def share(i, off, cc):
        return copy(piece(off, cc, None), shared, 0, i, pair)

    for d in (0, 1):
        far(d, d, 0).start()
    for d in (0, 1):
        far(d, 1 - d, 0).start()
    for d in (0, 1):
        near(d, 0).start()
    share(0, 0, c).start()
    for fetch in fetches:
        fetch.start()
    for d in (0, 1):
        far(d, d, -2 * SIGNS[d]).wait_recv()
        fourth(d, -2 * SIGNS[d]).start()
        third(d, d, -2 * SIGNS[d]).start()
    for d in (0, 1):
        far(d, 1 - d, -2 * SIGNS[d]).wait_recv()
        third(d, 1 - d, -2 * SIGNS[d]).start()
        share(1 + d, -2 * SIGNS[d], c).start()
    for d in (0, 1):
        near(d, -SIGNS[d]).wait_recv()
        share(3 + d, -SIGNS[d], c).start()
    for d in (0, 1):
        for half in (0, 1):
            third(d, half, -3 * SIGNS[d]).wait_recv()
        share(5 + d, -3 * SIGNS[d], c).start()
    for d in (0, 1):
        fourth(d, -4 * SIGNS[d]).wait_recv()
    share(7, 4, c).start()
    offsets = (0, -2, 2, -1, 1, -3, 3, 4)
    for i, off in enumerate(offsets):
        share(i, off, 1 - c).wait_recv()
    for d in (0, 1):
        for half in (0, 1):
            far(d, half, 0).wait_send()
            third(d, half, -2 * SIGNS[d]).wait_send()
        near(d, 0).wait_send()
        fourth(d, -2 * SIGNS[d]).wait_send()
    for i, off in enumerate(offsets):
        share(i, off, c).wait_send()
    for fetch in fetches:
        fetch.wait()


def z_gather(features, adj, rows, cols, nz):
    sem = pltpu.SemaphoreType.DMA
    return pl.pallas_call(
        functools.partial(z_gather_kernel, nz),
        out_shape=(
            jax.ShapeDtypeStruct((nz, 2, T, T), F32),
            jax.ShapeDtypeStruct(adj.shape, F32),
            jax.ShapeDtypeStruct(rows.shape, jnp.int32),
            jax.ShapeDtypeStruct(cols.shape, jnp.int32),
        ),
        in_specs=[HBM] * 4,
        out_specs=(VMEM,) * 4,
        scratch_shapes=[
            sem((2, 3)), sem((2, 3)), sem((2, 3)), sem((2, 3)), sem((1, 8)), sem((1, 8)), sem((4,)),
        ],
        compiler_params=pltpu.CompilerParams(collective_id=0, has_side_effects=True, vmem_limit_bytes=6 * MIB),
        name="z_gather",
    )(features, adj, rows, cols)


GROUP = 4

OFFSETS = (4, 3, -3, 2, -2, 1, -1, 0)


def position(off):
    return jnp.where(off >= 4, 2 * (off - 4), 7 - 2 * off)


def relative(tile_row, col, nx, ny):
    ahead_y = lax.rem(tile_row // nx - col // nx + ny, ny)
    ahead_x = lax.rem(lax.rem(tile_row, nx) - lax.rem(col, nx) + nx, nx)
    return (0, ahead_x, position(ahead_y)), (1, ahead_y, position(ahead_x))


def forward_kernel(ny, nx, rows, cols, count, adj, x, out, triple):
    col = lax.axis_index("col")
    out[...] = jnp.zeros_like(out)

    def prepare(c, carry):
        high, low = split(x[c])
        triple[c] = jnp.concatenate([high, high, low], axis=0)
        return carry

    lax.fori_loop(0, x.shape[0], prepare, 0)

    def group(g, carry):
        products = []
        for u in range(GROUP):
            s = g * GROUP + u
            high, low = split(adj[s])
            left = jnp.concatenate([high, low, high], axis=1)
            products.append(jnp.dot(left, triple[cols[s]], preferred_element_type=F32))
        for u in range(GROUP):
            for half, at in enumerate(relative(rows[g * GROUP + u], col, nx, ny)):
                out[at] = out[at] + products[u][half * (T // 2) : (half + 1) * (T // 2)]
        return carry

    lax.fori_loop(0, count[0] // GROUP, group, 0)


def forward(rows, cols, count, adj, x, ny, nx):
    return pl.pallas_call(
        functools.partial(forward_kernel, ny, nx),
        out_shape=jax.ShapeDtypeStruct((2, 8, 8, T // 2, T), F32),
        in_specs=[SMEM, SMEM, SMEM, VMEM, VMEM],
        out_specs=VMEM,
        scratch_shapes=[pltpu.VMEM((x.shape[0], 3 * T, T), BF16)],
        compiler_params=pltpu.CompilerParams(vmem_limit_bytes=14 * MIB),
        name="forward_tiles",
    )(rows, cols, count, adj, x)


def backward_kernel(ny, nx, rows, cols, count, adj, g, hidden, grad_weight, out, hidden_out, grad_weight_out, sem):
    col = lax.axis_index("col")
    stores = [
        pltpu.make_async_copy(hidden, hidden_out, sem.at[0]),
        pltpu.make_async_copy(grad_weight, grad_weight_out, sem.at[1]),
    ]
    for store in stores:
        store.start()
    out[...] = jnp.zeros_like(out)

    def group(i, carry):
        products = []
        for u in range(GROUP):
            s = i * GROUP + u
            upper, lower = relative(rows[s], col, nx, ny)
            products.append(dot3(jnp.concatenate([g[upper], g[lower]], axis=0), adj[s]))
        for u in range(GROUP):
            c = cols[i * GROUP + u]
            out[c] = out[c] + products[u]
        return carry

    lax.fori_loop(0, count[0] // GROUP, group, 0)
    for store in stores:
        store.wait()


def backward(rows, cols, count, adj, g, hidden, grad_weight, col_tiles, ny, nx):
    return pl.pallas_call(
        functools.partial(backward_kernel, ny, nx),
        out_shape=(
            jax.ShapeDtypeStruct((col_tiles, T, T), F32),
            jax.ShapeDtypeStruct(hidden.shape, F32),
            jax.ShapeDtypeStruct(grad_weight.shape, F32),
        ),
        in_specs=[SMEM, SMEM, SMEM, VMEM, VMEM, VMEM, VMEM],
        out_specs=(VMEM, HBM, HBM),
        scratch_shapes=[pltpu.SemaphoreType.DMA((2,))],
        compiler_params=pltpu.CompilerParams(vmem_limit_bytes=12 * MIB),
        name="backward_tiles",
    )(rows, cols, count, adj, g, hidden, grad_weight)


FAR, NEAR = 0, 1


def group(g):
    return pl.ds(4 * g, 4)


def opposite(m):
    return OFFSETS.index(4 if m == 0 else -OFFSETS[m])


def xy_kernel(
    ny, nx, nrow, partial, weight, cotangent, hidden, out, grad_weight,
    first, begun, later, joined, landed, lw, part_a, part_b, part_c, w_tall, w_wide,
    send1, recv1, send2, recv2, sendA, recvA, sendB, recvB, sendR, recvR, sendW, recvW,
):
    row, col = lax.axis_index("row"), lax.axis_index("col")
    y, x = col // nx, lax.rem(col, nx)
    quarter, half_rows = T // 4, T // 2
    wrows = T // nx

    def at_x(k):
        return (row, y * nx + wrap(x + k, nx))

    def at_y(k):
        return (row, wrap(y + k, ny) * nx + x)

    def at_row(k):
        return (lax.rem(row + k, nrow), col)

    along = (at_x, at_y)
    neighbour = [{sign: along[axis](sign) for sign in SIGNS} for axis in (0, 1)]
    greet([(nx - 1, at_x), (ny - 1, at_y), (nrow - 1, at_row)])

    def loop(start, stop, body):
        def step(k, carry):
            body(k)
            return carry
        lax.fori_loop(start, stop, step, 0)

    both = ((0, 0), (1, 0), (0, 1), (1, 1))

    def quarter_of(d):
        return pl.ds(d * quarter, quarter)

    def move(axis, d, s, g):
        tiles = group(g)
        if s == 0:
            src, dst = partial.at[axis, 4, tiles, quarter_of(d), :], first.at[axis, d, tiles]
        elif s == 1:
            src, dst = begun.at[axis, d, tiles], later.at[axis, d, 0, tiles]
        else:
            src, dst = later.at[axis, d, s - 2, tiles], later.at[axis, d, s - 1, tiles]
        return remote(src, dst, send1.at[axis, d, s, g], recv1.at[axis, d, s, g], neighbour[axis][SIGNS[d]])

    def hop(axis, d, s, g):
        if s > 0:
            tiles = group(g)
            mine = partial[axis, (4 - s) * SIGNS[d] % 8, tiles]
            if s == 1:
                begun[axis, d, tiles] = mine
                move(axis, d, 0, g).wait_recv()
                begun[axis, d, tiles, quarter_of(d), :] = begun[axis, d, tiles, quarter_of(d), :] + first[axis, d, tiles]
            else:
                move(axis, d, s - 1, g).wait_recv()
                later[axis, d, s - 2, tiles] = later[axis, d, s - 2, tiles] + mine
        move(axis, d, s, g).start()

    def part(axis, m):
        return remote(
            joined.at[axis, m], landed.at[axis, m], send2.at[axis, m], recv2.at[axis, m], along[1 - axis](OFFSETS[m])
        )

    def finish(axis, g):
        tiles = group(g)
        for d in (0, 1):
            move(axis, d, 3, g).wait_recv()
        joined[axis, tiles] = partial[axis, 0, tiles] + later[axis, 0, 2, tiles] + later[axis, 1, 2, tiles]
        for m in range(4 * g, 4 * g + 4):
            if OFFSETS[m] != 0:
                part(axis, m).start()

    for s in range(4):
        for g in (FAR, NEAR):
            for axis, d in both:
                hop(axis, d, s, g)
        if s == 0:
            high, low = split(weight[...])
            w_tall[...] = jnp.concatenate([high, high, low], axis=0)
            w_wide[...] = jnp.concatenate([high, low, high], axis=1)
    for g in (FAR, NEAR):
        for axis in (0, 1):
            finish(axis, g)
    sums = []
    for axis in (0, 1):
        total = joined[axis, 7]
        for m in range(7):
            part(axis, m).wait_recv()
            total = total + landed[axis, m]
        sums.append(total)
    summed = jnp.concatenate(sums, axis=0)

    high, low = split(summed)
    value = jnp.dot(jnp.concatenate([high, low, high], axis=1), w_tall[...], preferred_element_type=F32)
    scale = 0.7978845608028654
    t = jnp.tanh(scale * (value + 0.044715 * value * value * value))
    slope = 0.5 * (1.0 + t) + 0.5 * value * (1.0 - t * t) * scale * (1.0 + 3.0 * 0.044715 * value * value)
    pre = cotangent[...] * slope
    high, low = split(pre)
    mixed = lax.dot_general(
        w_wide[...], jnp.concatenate([high, high, low], axis=1), (((1,), (1,)), ((), ())), preferred_element_type=F32
    )
    for axis in (0, 1):
        out[axis, 0, 7] = mixed[axis * half_rows : (axis + 1) * half_rows]

    def spread(axis, m):
        ref = out.at[axis, 0, 7]
        return remote(
            ref, out.at[axis, 0, opposite(m)], sendA.at[axis, m], recvA.at[axis, opposite(m)], along[1 - axis](OFFSETS[m])
        )

    def spread_in(axis, m):
        ref = out.at[axis, 0, m]
        return remote(ref, ref, sendA.at[axis, m], recvA.at[axis, m], along[1 - axis](OFFSETS[m]))

    def relay(axis, d, s, g):
        sign = SIGNS[d]
        tiles = group(g)
        rows = quarter_of(d) if s == 3 else slice(None)
        src = out.at[axis, -sign * s % 8, tiles, rows, :]
        dst = out.at[axis, -sign * (s + 1) % 8, tiles, rows, :]
        return remote(src, dst, sendB.at[axis, d, s, g], recvB.at[axis, d, s, g], neighbour[axis][sign])

    def hand_on(s, g):
        for axis, d in both:
            if s > 0:
                relay(axis, d, s - 1, g).wait_recv()
            relay(axis, d, s, g).start()

    for m in (6, 5, 4, 3, 2, 1, 0):
        for axis in (0, 1):
            spread(axis, m).start()

    hidden[...] = 0.5 * value * (1.0 + t)
    lw[...] = dot3(summed.T, pre)

    def weight_rows(k):
        return pl.ds(pl.multiple_of(k * wrows, wrows), wrows)

    def scatter(k):
        return remote(lw.at[weight_rows(wrap(x + k, nx)), :], part_a.at[x], sendR.at[0, k], recvR.at[0, k], at_x(k))

    def scatter_in(k):
        slot = part_a.at[wrap(x - k, nx)]
        return remote(slot, slot, sendR.at[0, k], recvR.at[0, k], at_x(k))

    def swap_y(k):
        return remote(part_b.at[y], part_b.at[y], sendR.at[1, k], recvR.at[1, k], at_y(k))

    def swap_y_in(k):
        slot = part_b.at[wrap(y - k, ny)]
        return remote(slot, slot, sendR.at[1, k], recvR.at[1, k], at_y(k))

    def swap_row(k):
        return remote(part_c.at[row], part_c.at[row], sendW.at[k], recvW.at[k], at_row(k))

    def swap_row_in(k):
        slot = part_c.at[wrap(row - k, nrow)]
        return remote(slot, slot, sendW.at[k], recvW.at[k], at_row(k))

    def final(k):
        ref = grad_weight.at[weight_rows(x), :]
        return remote(ref, ref, sendR.at[2, k], recvR.at[2, k], at_x(k))

    def final_in(k):
        ref = grad_weight.at[weight_rows(wrap(x - k, nx)), :]
        return remote(ref, ref, sendR.at[2, k], recvR.at[2, k], at_x(k))

    def add_up(slots, n):
        total = slots[0]
        for k in range(1, n):
            total = total + slots[k]
        return total

    part_a[x] = lw[weight_rows(x), :]
    loop(1, nx, lambda k: scatter(k).start())
    for m in (6, 5, 4):
        for axis in (0, 1):
            spread_in(axis, m).wait_recv()
    hand_on(0, NEAR)
    for m in (3, 2, 1, 0):
        for axis in (0, 1):
            spread_in(axis, m).wait_recv()
    hand_on(0, FAR)
    loop(1, nx, lambda k: scatter_in(k).wait_recv())
    part_b[y] = add_up(part_a, nx)
    loop(1, ny, lambda k: swap_y(k).start())
    hand_on(1, NEAR)
    hand_on(1, FAR)
    loop(1, ny, lambda k: swap_y_in(k).wait_recv())
    part_c[row] = add_up(part_b, ny)
    loop(1, nrow, lambda k: swap_row(k).start())
    hand_on(2, NEAR)
    hand_on(2, FAR)
    loop(1, nrow, lambda k: swap_row_in(k).wait_recv())
    grad_weight[weight_rows(x), :] = add_up(part_c, nrow)
    loop(1, nx, lambda k: final(k).start())
    hand_on(3, NEAR)
    hand_on(3, FAR)
    for g in (NEAR, FAR):
        for axis, d in both:
            relay(axis, d, 3, g).wait_recv()
    loop(1, nx, lambda k: final_in(k).wait_recv())

    for g in (FAR, NEAR):
        for axis, d in both:
            for s in range(4):
                move(axis, d, s, g).wait_send()
                relay(axis, d, s, g).wait_send()
    for axis in (0, 1):
        for m in range(7):
            part(axis, m).wait_send()
            spread(axis, m).wait_send()
    loop(1, nx, lambda k: scatter(k).wait_send())
    loop(1, ny, lambda k: swap_y(k).wait_send())
    loop(1, nrow, lambda k: swap_row(k).wait_send())
    loop(1, nx, lambda k: final(k).wait_send())


def xy(partial, weight, cotangent, ny, nx, nrow):
    sem = pltpu.SemaphoreType.DMA
    half, wrows = T // 2, T // nx
    return pl.pallas_call(
        functools.partial(xy_kernel, ny, nx, nrow),
        out_shape=(
            jax.ShapeDtypeStruct((T, T), F32),
            jax.ShapeDtypeStruct((2, 8, 8, half, T), F32),
            jax.ShapeDtypeStruct((T, T), F32),
        ),
        in_specs=[VMEM] * 3,
        out_specs=(VMEM,) * 3,
        scratch_shapes=[
            pltpu.VMEM((2, 2, 8, T // 4, T), F32),
            pltpu.VMEM((2, 2, 8, half, T), F32),
            pltpu.VMEM((2, 2, 3, 8, half, T), F32),
            pltpu.VMEM((2, 8, half, T), F32),
            pltpu.VMEM((2, 7, half, T), F32),
            pltpu.VMEM((T, T), F32),
            pltpu.VMEM((nx, wrows, T), F32),
            pltpu.VMEM((ny, wrows, T), F32),
            pltpu.VMEM((nrow, wrows, T), F32),
            pltpu.VMEM((3 * T, T), BF16),
            pltpu.VMEM((T, 3 * T), BF16),
            sem((2, 2, 4, 2)), sem((2, 2, 4, 2)),
            sem((2, 8)), sem((2, 8)),
            sem((2, 8)), sem((2, 8)),
            sem((2, 2, 4, 2)), sem((2, 2, 4, 2)),
            sem((3, 8)), sem((3, 8)),
            sem((nrow,)), sem((nrow,)),
        ],
        compiler_params=pltpu.CompilerParams(collective_id=1, has_side_effects=True, vmem_limit_bytes=20 * MIB),
        name="xy_exchange",
    )(partial, weight, cotangent)


def z_scatter_kernel(
    nz, part, out, other, acc, near_buf, relay_buf, third_buf, fourth_buf,
    pair_send, pair_recv, send, recv,
):
    row, col = lax.axis_index("row"), lax.axis_index("col")
    z, c = row // 2, lax.rem(row, 2)
    half_rows = T // 2
    ring = ring_peers(z, c, col, nz)
    pair = (z * 2 + 1 - c, col)
    greet([(1, lambda k, to=to: to) for to in (*ring.values(), pair)])

    def give(off):
        zz = wrap(z + off, nz)
        return remote(part.at[zz, 1 - c], other.at[zz], pair_send.at[off % nz], pair_recv.at[off % nz], pair)

    order = (4, 3, -3, 2, -2, 1, -1, 0)
    for off in order:
        give(off).start()

    def term(off):
        give(off).wait_recv()
        zz = wrap(z + off, nz)
        return part[zz, c] + other[zz]

    def copy(src, dst, d, kind, distance):
        return remote(src, dst, send.at[d, kind], recv.at[d, kind], ring[distance * SIGNS[d]])

    def fourth(d):
        return copy(acc.at[4, pl.ds(d * half_rows, half_rows), :], fourth_buf.at[d], d, 0, 2)

    def third(d):
        return copy(acc.at[2 + d], third_buf.at[d], d, 1, 1)

    def relay(d):
        return copy(acc.at[d], relay_buf.at[d], d, 2, 2)

    def near(d):
        return copy(acc.at[5 + d], near_buf.at[d], d, 3, 1)

    acc[4] = term(4)
    for d in (0, 1):
        fourth(d).start()
    for d in (0, 1):
        acc[2 + d] = term(3 * SIGNS[d])
        third(d).start()
    for d in (0, 1):
        acc[d] = term(2 * SIGNS[d])
    for d in (0, 1):
        acc[5 + d] = term(SIGNS[d])
        near(d).start()
    mine = term(0)
    for d in (0, 1):
        third(d).wait_recv()
        acc[d] = acc[d] + third_buf[d]
        fourth(d).wait_recv()
        here = pl.ds(d * half_rows, half_rows)
        acc[d, here, :] = acc[d, here, :] + fourth_buf[d]
        relay(d).start()
    for d in (0, 1):
        near(d).wait_recv()
        mine = mine + near_buf[d]
    for d in (0, 1):
        relay(d).wait_recv()
        mine = mine + relay_buf[d]
    out[...] = mine
    for off in order:
        give(off).wait_send()
    for d in (0, 1):
        fourth(d).wait_send()
        third(d).wait_send()
        relay(d).wait_send()
        near(d).wait_send()


def z_scatter(part, nz):
    sem = pltpu.SemaphoreType.DMA
    return pl.pallas_call(
        functools.partial(z_scatter_kernel, nz),
        out_shape=jax.ShapeDtypeStruct((T, T), F32),
        in_specs=[VMEM],
        out_specs=VMEM,
        scratch_shapes=[
            pltpu.VMEM((nz, T, T), F32),
            pltpu.VMEM((7, T, T), F32),
            pltpu.VMEM((2, T, T), F32),
            pltpu.VMEM((2, T, T), F32),
            pltpu.VMEM((2, T, T), F32),
            pltpu.VMEM((2, T // 2, T), F32),
            sem((nz,)), sem((nz,)),
            sem((2, 4)), sem((2, 4)),
        ],
        compiler_params=pltpu.CompilerParams(collective_id=2, has_side_effects=True, vmem_limit_bytes=6 * MIB),
        name="z_scatter",
    )(part.reshape(nz, 2, T, T))


def local(nrow, ncol, features, weight, adj_tiles, tile_row, tile_col, slot_count, cotangent):
    nz, nx = nrow // 2, NX
    ny = ncol // nx
    rows, cols, count, adj = tile_row[0, 0], tile_col[0, 0], slot_count[0], adj_tiles[0, 0]
    in_hbm = [pltpu.with_memory_space_constraint(a, pltpu.HBM) for a in (features, adj, rows, cols)]
    x, adj, rows, cols = z_gather(*in_hbm, nz)
    partial = forward(rows, cols, count, adj, x.reshape(nrow, T, T), ny, nx)
    hidden, pre_rows, grad_weight = xy(partial, weight, cotangent, ny, nx, nrow)
    part, hidden, grad_weight = backward(rows, cols, count, adj, pre_rows, hidden, grad_weight, nrow, ny, nx)
    return hidden, z_scatter(part, nz).T, grad_weight


def solution(mesh):
    placed = (
        P(("col", "row"), None),
        P(),
        P("row", "col", None, None, None),
        P("row", "col", None),
        P("row", "col", None),
        P("row", "col"),
        P(("row", "col"), None),
    )
    return jax.shard_map(
        functools.partial(local, mesh.shape["row"], mesh.shape["col"]),
        mesh=mesh,
        in_specs=placed,
        out_specs=(P(("row", "col"), None), P(("col", "row"), None), P()),
        check_vma=False,
    )
```

```python
import functools
import jax
import jax.numpy as jnp
from jax import lax
from jax.experimental import pallas as pl
from jax.experimental.pallas import tpu as pltpu
from jax.sharding import PartitionSpec as P

MESH = pl.DeviceIdType.MESH
T = 128
NX = 8
F32 = jnp.float32
BF16 = jnp.bfloat16
VMEM = pl.BlockSpec(memory_space=pltpu.VMEM)
SMEM = pl.BlockSpec(memory_space=pltpu.SMEM)
HBM = pl.BlockSpec(memory_space=pltpu.HBM)
MIB = 1024 * 1024


def split(value):
    high = value.astype(BF16)
    low = (value - high.astype(F32)).astype(BF16)
    return high, low


def dot3(left, right):
    lh, ll = split(left)
    rh, rl = split(right)
    return jnp.dot(
        jnp.concatenate([lh, ll, lh], axis=1),
        jnp.concatenate([rh, rh, rl], axis=0),
        preferred_element_type=F32,
    )


def wrap(index, n):
    return lax.rem(index + n, n)


def greet(peers):
    barrier = pltpu.get_barrier_semaphore()
    total = 0
    for count, device in peers:
        def one(k, carry, device=device):
            pl.semaphore_signal(barrier, inc=1, device_id=device(k), device_id_type=MESH)
            return carry
        lax.fori_loop(1, count + 1, one, 0)
        total += count
    pl.semaphore_wait(barrier, total)


def remote(src, dst, send, recv, device):
    return pltpu.make_async_remote_copy(
        src_ref=src, dst_ref=dst, send_sem=send, recv_sem=recv, device_id=device, device_id_type=MESH
    )


SIGNS = (1, -1)


def ring_peers(z, c, col, nz):
    return {k: (wrap(z + k, nz) * 2 + c, col) for k in (1, -1, 2, -2)}


def z_gather_kernel(
    nz, x_ref, adj, rows, cols, out_ref, adj_out, rows_out, cols_out,
    send, recv, relay_send, relay_recv, pair_send, pair_recv, fetch_sem,
):
    row, col = lax.axis_index("row"), lax.axis_index("col")
    z, c = row // 2, lax.rem(row, 2)
    half_rows = T // 2
    ring = ring_peers(z, c, col, nz)
    pair = (z * 2 + 1 - c, col)
    own = pltpu.make_async_copy(x_ref, out_ref.at[z, c], fetch_sem.at[0])
    own.start()
    fetches = [
        pltpu.make_async_copy(src, dst, fetch_sem.at[i])
        for i, (src, dst) in enumerate(((adj, adj_out), (rows, rows_out), (cols, cols_out)), 1)
    ]
    greet([(1, lambda k, to=to: to) for to in (*ring.values(), pair)])
    own.wait()

    def piece(off, cc, half):
        ref = out_ref.at[wrap(z + off, nz), cc]
        return ref if half is None else ref.at[pl.ds(half * half_rows, half_rows), :]

    def copy(ref, sems, i, j, to):
        return remote(ref, ref, sems[0].at[i, j], sems[1].at[i, j], to)

    first, second, shared = (send, recv), (relay_send, relay_recv), (pair_send, pair_recv)

    def far(d, half, off):
        return copy(piece(off, c, half), first, d, half, ring[2 * SIGNS[d]])

    def near(d, off):
        return copy(piece(off, c, None), first, d, 2, ring[SIGNS[d]])

    def third(d, half, off):
        return copy(piece(off, c, half), second, d, half, ring[SIGNS[d]])

    def fourth(d, off):
        return copy(piece(off, c, d), second, d, 2, ring[2 * SIGNS[d]])

    def share(i, off, cc):
        return copy(piece(off, cc, None), shared, 0, i, pair)

    for d in (0, 1):
        far(d, d, 0).start()
    for d in (0, 1):
        far(d, 1 - d, 0).start()
    for d in (0, 1):
        near(d, 0).start()
    share(0, 0, c).start()
    for fetch in fetches:
        fetch.start()
    for d in (0, 1):
        far(d, d, -2 * SIGNS[d]).wait_recv()
        fourth(d, -2 * SIGNS[d]).start()
        third(d, d, -2 * SIGNS[d]).start()
    for d in (0, 1):
        far(d, 1 - d, -2 * SIGNS[d]).wait_recv()
        third(d, 1 - d, -2 * SIGNS[d]).start()
        share(1 + d, -2 * SIGNS[d], c).start()
    for d in (0, 1):
        near(d, -SIGNS[d]).wait_recv()
        share(3 + d, -SIGNS[d], c).start()
    for d in (0, 1):
        for half in (0, 1):
            third(d, half, -3 * SIGNS[d]).wait_recv()
        share(5 + d, -3 * SIGNS[d], c).start()
    for d in (0, 1):
        fourth(d, -4 * SIGNS[d]).wait_recv()
    share(7, 4, c).start()
    offsets = (0, -2, 2, -1, 1, -3, 3, 4)
    for i, off in enumerate(offsets):
        share(i, off, 1 - c).wait_recv()
    for d in (0, 1):
        for half in (0, 1):
            far(d, half, 0).wait_send()
            third(d, half, -2 * SIGNS[d]).wait_send()
        near(d, 0).wait_send()
        fourth(d, -2 * SIGNS[d]).wait_send()
    for i, off in enumerate(offsets):
        share(i, off, c).wait_send()
    for fetch in fetches:
        fetch.wait()


def z_gather(features, adj, rows, cols, nz):
    sem = pltpu.SemaphoreType.DMA
    return pl.pallas_call(
        functools.partial(z_gather_kernel, nz),
        out_shape=(
            jax.ShapeDtypeStruct((nz, 2, T, T), F32),
            jax.ShapeDtypeStruct(adj.shape, F32),
            jax.ShapeDtypeStruct(rows.shape, jnp.int32),
            jax.ShapeDtypeStruct(cols.shape, jnp.int32),
        ),
        in_specs=[HBM] * 4,
        out_specs=(VMEM,) * 4,
        scratch_shapes=[
            sem((2, 3)), sem((2, 3)), sem((2, 3)), sem((2, 3)), sem((1, 8)), sem((1, 8)), sem((4,)),
        ],
        compiler_params=pltpu.CompilerParams(collective_id=0, has_side_effects=True, vmem_limit_bytes=6 * MIB),
        name="z_gather",
    )(features, adj, rows, cols)


GROUP = 8

OFFSETS = (4, 3, -3, 2, -2, 1, -1, 0)


def position(off):
    return jnp.where(off >= 4, 2 * (off - 4), 7 - 2 * off)


def relative(tile_row, col, nx, ny):
    ahead_y = lax.rem(tile_row // nx - col // nx + ny, ny)
    ahead_x = lax.rem(lax.rem(tile_row, nx) - lax.rem(col, nx) + nx, nx)
    return (0, ahead_x, position(ahead_y)), (1, ahead_y, position(ahead_x))


def forward_kernel(ny, nx, rows, cols, count, adj, x, out, triple):
    col = lax.axis_index("col")
    out[...] = jnp.zeros_like(out)

    def prepare(c, carry):
        high, low = split(x[c])
        triple[c] = jnp.concatenate([high, high, low], axis=0)
        return carry

    lax.fori_loop(0, x.shape[0], prepare, 0)

    def group(g, carry):
        products = []
        for u in range(GROUP):
            s = g * GROUP + u
            high, low = split(adj[s])
            left = jnp.concatenate([high, low, high], axis=1)
            product = jnp.dot(left, triple[cols[s]], preferred_element_type=F32)
            products.append(jnp.where(s < count[0], product, 0.0))
        for u in range(GROUP):
            for half, at in enumerate(relative(rows[g * GROUP + u], col, nx, ny)):
                out[at] = out[at] + products[u][half * (T // 2) : (half + 1) * (T // 2)]
        return carry

    lax.fori_loop(0, (count[0] + GROUP - 1) // GROUP, group, 0)


def forward(rows, cols, count, adj, x, ny, nx):
    return pl.pallas_call(
        functools.partial(forward_kernel, ny, nx),
        out_shape=jax.ShapeDtypeStruct((2, 8, 8, T // 2, T), F32),
        in_specs=[SMEM, SMEM, SMEM, VMEM, VMEM],
        out_specs=VMEM,
        scratch_shapes=[pltpu.VMEM((x.shape[0], 3 * T, T), BF16)],
        compiler_params=pltpu.CompilerParams(vmem_limit_bytes=14 * MIB),
        name="forward_tiles",
    )(rows, cols, count, adj, x)


def backward_kernel(ny, nx, rows, cols, count, adj, g, hidden, grad_weight, out, hidden_out, grad_weight_out, sem):
    col = lax.axis_index("col")
    stores = [
        pltpu.make_async_copy(hidden, hidden_out, sem.at[0]),
        pltpu.make_async_copy(grad_weight, grad_weight_out, sem.at[1]),
    ]
    for store in stores:
        store.start()
    out[...] = jnp.zeros_like(out)

    def group(i, carry):
        products = []
        for u in range(GROUP):
            s = i * GROUP + u
            upper, lower = relative(rows[s], col, nx, ny)
            product = dot3(jnp.concatenate([g[upper], g[lower]], axis=0), adj[s])
            products.append(jnp.where(s < count[0], product, 0.0))
        for u in range(GROUP):
            c = cols[i * GROUP + u]
            out[c] = out[c] + products[u]
        return carry

    lax.fori_loop(0, (count[0] + GROUP - 1) // GROUP, group, 0)
    for store in stores:
        store.wait()


def backward(rows, cols, count, adj, g, hidden, grad_weight, col_tiles, ny, nx):
    return pl.pallas_call(
        functools.partial(backward_kernel, ny, nx),
        out_shape=(
            jax.ShapeDtypeStruct((col_tiles, T, T), F32),
            jax.ShapeDtypeStruct(hidden.shape, F32),
            jax.ShapeDtypeStruct(grad_weight.shape, F32),
        ),
        in_specs=[SMEM, SMEM, SMEM, VMEM, VMEM, VMEM, VMEM],
        out_specs=(VMEM, HBM, HBM),
        scratch_shapes=[pltpu.SemaphoreType.DMA((2,))],
        compiler_params=pltpu.CompilerParams(vmem_limit_bytes=12 * MIB),
        name="backward_tiles",
    )(rows, cols, count, adj, g, hidden, grad_weight)


FAR, NEAR = 0, 1


def group(g):
    return pl.ds(4 * g, 4)


def opposite(m):
    return OFFSETS.index(4 if m == 0 else -OFFSETS[m])


def xy_kernel(
    ny, nx, nrow, partial, weight, cotangent, hidden, out, grad_weight,
    first, begun, later, joined, landed, lw, part_a, part_b, part_c, w_tall, w_wide,
    send1, recv1, send2, recv2, sendA, recvA, sendB, recvB, sendR, recvR, sendW, recvW,
):
    row, col = lax.axis_index("row"), lax.axis_index("col")
    y, x = col // nx, lax.rem(col, nx)
    quarter, half_rows = T // 4, T // 2
    wrows = T // nx

    def at_x(k):
        return (row, y * nx + wrap(x + k, nx))

    def at_y(k):
        return (row, wrap(y + k, ny) * nx + x)

    def at_row(k):
        return (lax.rem(row + k, nrow), col)

    along = (at_x, at_y)
    neighbour = [{sign: along[axis](sign) for sign in SIGNS} for axis in (0, 1)]
    greet([(nx - 1, at_x), (ny - 1, at_y), (nrow - 1, at_row)])

    def loop(start, stop, body):
        def step(k, carry):
            body(k)
            return carry
        lax.fori_loop(start, stop, step, 0)

    both = ((0, 0), (1, 0), (0, 1), (1, 1))

    def quarter_of(d):
        return pl.ds(d * quarter, quarter)

    def move(axis, d, s, g):
        tiles = group(g)
        if s == 0:
            src, dst = partial.at[axis, 4, tiles, quarter_of(d), :], first.at[axis, d, tiles]
        elif s == 1:
            src, dst = begun.at[axis, d, tiles], later.at[axis, d, 0, tiles]
        else:
            src, dst = later.at[axis, d, s - 2, tiles], later.at[axis, d, s - 1, tiles]
        return remote(src, dst, send1.at[axis, d, s, g], recv1.at[axis, d, s, g], neighbour[axis][SIGNS[d]])

    def hop(axis, d, s, g):
        if s > 0:
            tiles = group(g)
            mine = partial[axis, (4 - s) * SIGNS[d] % 8, tiles]
            if s == 1:
                begun[axis, d, tiles] = mine
                move(axis, d, 0, g).wait_recv()
                begun[axis, d, tiles, quarter_of(d), :] = begun[axis, d, tiles, quarter_of(d), :] + first[axis, d, tiles]
            else:
                move(axis, d, s - 1, g).wait_recv()
                later[axis, d, s - 2, tiles] = later[axis, d, s - 2, tiles] + mine
        move(axis, d, s, g).start()

    def part(axis, m):
        return remote(
            joined.at[axis, m], landed.at[axis, m], send2.at[axis, m], recv2.at[axis, m], along[1 - axis](OFFSETS[m])
        )

    def finish(axis, g):
        tiles = group(g)
        for d in (0, 1):
            move(axis, d, 3, g).wait_recv()
        joined[axis, tiles] = partial[axis, 0, tiles] + later[axis, 0, 2, tiles] + later[axis, 1, 2, tiles]
        for m in range(4 * g, 4 * g + 4):
            if OFFSETS[m] != 0:
                part(axis, m).start()

    for s in range(4):
        for g in (FAR, NEAR):
            for axis, d in both:
                hop(axis, d, s, g)
        if s == 0:
            high, low = split(weight[...])
            w_tall[...] = jnp.concatenate([high, high, low], axis=0)
            w_wide[...] = jnp.concatenate([high, low, high], axis=1)
    for g in (FAR, NEAR):
        for axis in (0, 1):
            finish(axis, g)
    sums = []
    for axis in (0, 1):
        total = joined[axis, 7]
        for m in range(7):
            part(axis, m).wait_recv()
            total = total + landed[axis, m]
        sums.append(total)
    summed = jnp.concatenate(sums, axis=0)

    high, low = split(summed)
    value = jnp.dot(jnp.concatenate([high, low, high], axis=1), w_tall[...], preferred_element_type=F32)
    scale = 0.7978845608028654
    t = jnp.tanh(scale * (value + 0.044715 * value * value * value))
    slope = 0.5 * (1.0 + t) + 0.5 * value * (1.0 - t * t) * scale * (1.0 + 3.0 * 0.044715 * value * value)
    pre = cotangent[...] * slope
    high, low = split(pre)
    mixed = lax.dot_general(
        w_wide[...], jnp.concatenate([high, high, low], axis=1), (((1,), (1,)), ((), ())), preferred_element_type=F32
    )
    for axis in (0, 1):
        out[axis, 0, 7] = mixed[axis * half_rows : (axis + 1) * half_rows]

    def spread(axis, m):
        ref = out.at[axis, 0, 7]
        return remote(
            ref, out.at[axis, 0, opposite(m)], sendA.at[axis, m], recvA.at[axis, opposite(m)], along[1 - axis](OFFSETS[m])
        )

    def spread_in(axis, m):
        ref = out.at[axis, 0, m]
        return remote(ref, ref, sendA.at[axis, m], recvA.at[axis, m], along[1 - axis](OFFSETS[m]))

    def relay(axis, d, s, g):
        sign = SIGNS[d]
        tiles = group(g)
        rows = quarter_of(d) if s == 3 else slice(None)
        src = out.at[axis, -sign * s % 8, tiles, rows, :]
        dst = out.at[axis, -sign * (s + 1) % 8, tiles, rows, :]
        return remote(src, dst, sendB.at[axis, d, s, g], recvB.at[axis, d, s, g], neighbour[axis][sign])

    def hand_on(s, g):
        for axis, d in both:
            if s > 0:
                relay(axis, d, s - 1, g).wait_recv()
            relay(axis, d, s, g).start()

    for m in (6, 5, 4, 3, 2, 1, 0):
        for axis in (0, 1):
            spread(axis, m).start()

    hidden[...] = 0.5 * value * (1.0 + t)
    lw[...] = dot3(summed.T, pre)

    def weight_rows(k):
        return pl.ds(pl.multiple_of(k * wrows, wrows), wrows)

    def scatter(k):
        return remote(lw.at[weight_rows(wrap(x + k, nx)), :], part_a.at[x], sendR.at[0, k], recvR.at[0, k], at_x(k))

    def scatter_in(k):
        slot = part_a.at[wrap(x - k, nx)]
        return remote(slot, slot, sendR.at[0, k], recvR.at[0, k], at_x(k))

    def swap_y(k):
        return remote(part_b.at[y], part_b.at[y], sendR.at[1, k], recvR.at[1, k], at_y(k))

    def swap_y_in(k):
        slot = part_b.at[wrap(y - k, ny)]
        return remote(slot, slot, sendR.at[1, k], recvR.at[1, k], at_y(k))

    def swap_row(k):
        return remote(part_c.at[row], part_c.at[row], sendW.at[k], recvW.at[k], at_row(k))

    def swap_row_in(k):
        slot = part_c.at[wrap(row - k, nrow)]
        return remote(slot, slot, sendW.at[k], recvW.at[k], at_row(k))

    def final(k):
        ref = grad_weight.at[weight_rows(x), :]
        return remote(ref, ref, sendR.at[2, k], recvR.at[2, k], at_x(k))

    def final_in(k):
        ref = grad_weight.at[weight_rows(wrap(x - k, nx)), :]
        return remote(ref, ref, sendR.at[2, k], recvR.at[2, k], at_x(k))

    def add_up(slots, n):
        total = slots[0]
        for k in range(1, n):
            total = total + slots[k]
        return total

    part_a[x] = lw[weight_rows(x), :]
    loop(1, nx, lambda k: scatter(k).start())
    for m in (6, 5, 4):
        for axis in (0, 1):
            spread_in(axis, m).wait_recv()
    hand_on(0, NEAR)
    for m in (3, 2, 1, 0):
        for axis in (0, 1):
            spread_in(axis, m).wait_recv()
    hand_on(0, FAR)
    loop(1, nx, lambda k: scatter_in(k).wait_recv())
    part_b[y] = add_up(part_a, nx)
    loop(1, ny, lambda k: swap_y(k).start())
    hand_on(1, NEAR)
    hand_on(1, FAR)
    loop(1, ny, lambda k: swap_y_in(k).wait_recv())
    part_c[row] = add_up(part_b, ny)
    loop(1, nrow, lambda k: swap_row(k).start())
    hand_on(2, NEAR)
    hand_on(2, FAR)
    loop(1, nrow, lambda k: swap_row_in(k).wait_recv())
    grad_weight[weight_rows(x), :] = add_up(part_c, nrow)
    loop(1, nx, lambda k: final(k).start())
    hand_on(3, NEAR)
    hand_on(3, FAR)
    for g in (NEAR, FAR):
        for axis, d in both:
            relay(axis, d, 3, g).wait_recv()
    loop(1, nx, lambda k: final_in(k).wait_recv())

    for g in (FAR, NEAR):
        for axis, d in both:
            for s in range(4):
                move(axis, d, s, g).wait_send()
                relay(axis, d, s, g).wait_send()
    for axis in (0, 1):
        for m in range(7):
            part(axis, m).wait_send()
            spread(axis, m).wait_send()
    loop(1, nx, lambda k: scatter(k).wait_send())
    loop(1, ny, lambda k: swap_y(k).wait_send())
    loop(1, nrow, lambda k: swap_row(k).wait_send())
    loop(1, nx, lambda k: final(k).wait_send())


def xy(partial, weight, cotangent, ny, nx, nrow):
    sem = pltpu.SemaphoreType.DMA
    half, wrows = T // 2, T // nx
    return pl.pallas_call(
        functools.partial(xy_kernel, ny, nx, nrow),
        out_shape=(
            jax.ShapeDtypeStruct((T, T), F32),
            jax.ShapeDtypeStruct((2, 8, 8, half, T), F32),
            jax.ShapeDtypeStruct((T, T), F32),
        ),
        in_specs=[VMEM] * 3,
        out_specs=(VMEM,) * 3,
        scratch_shapes=[
            pltpu.VMEM((2, 2, 8, T // 4, T), F32),
            pltpu.VMEM((2, 2, 8, half, T), F32),
            pltpu.VMEM((2, 2, 3, 8, half, T), F32),
            pltpu.VMEM((2, 8, half, T), F32),
            pltpu.VMEM((2, 7, half, T), F32),
            pltpu.VMEM((T, T), F32),
            pltpu.VMEM((nx, wrows, T), F32),
            pltpu.VMEM((ny, wrows, T), F32),
            pltpu.VMEM((nrow, wrows, T), F32),
            pltpu.VMEM((3 * T, T), BF16),
            pltpu.VMEM((T, 3 * T), BF16),
            sem((2, 2, 4, 2)), sem((2, 2, 4, 2)),
            sem((2, 8)), sem((2, 8)),
            sem((2, 8)), sem((2, 8)),
            sem((2, 2, 4, 2)), sem((2, 2, 4, 2)),
            sem((3, 8)), sem((3, 8)),
            sem((nrow,)), sem((nrow,)),
        ],
        compiler_params=pltpu.CompilerParams(collective_id=1, has_side_effects=True, vmem_limit_bytes=20 * MIB),
        name="xy_exchange",
    )(partial, weight, cotangent)


def z_scatter_kernel(
    nz, part, out, other, acc, near_buf, relay_buf, third_buf, fourth_buf,
    pair_send, pair_recv, send, recv,
):
    row, col = lax.axis_index("row"), lax.axis_index("col")
    z, c = row // 2, lax.rem(row, 2)
    half_rows = T // 2
    ring = ring_peers(z, c, col, nz)
    pair = (z * 2 + 1 - c, col)
    greet([(1, lambda k, to=to: to) for to in (*ring.values(), pair)])

    def give(off):
        zz = wrap(z + off, nz)
        return remote(part.at[zz, 1 - c], other.at[zz], pair_send.at[off % nz], pair_recv.at[off % nz], pair)

    order = (4, 3, -3, 2, -2, 1, -1, 0)
    for off in order:
        give(off).start()

    def term(off):
        give(off).wait_recv()
        zz = wrap(z + off, nz)
        return part[zz, c] + other[zz]

    def copy(src, dst, d, kind, distance):
        return remote(src, dst, send.at[d, kind], recv.at[d, kind], ring[distance * SIGNS[d]])

    def fourth(d):
        return copy(acc.at[4, pl.ds(d * half_rows, half_rows), :], fourth_buf.at[d], d, 0, 2)

    def third(d):
        return copy(acc.at[2 + d], third_buf.at[d], d, 1, 1)

    def relay(d):
        return copy(acc.at[d], relay_buf.at[d], d, 2, 2)

    def near(d):
        return copy(acc.at[5 + d], near_buf.at[d], d, 3, 1)

    acc[4] = term(4)
    for d in (0, 1):
        fourth(d).start()
    for d in (0, 1):
        acc[2 + d] = term(3 * SIGNS[d])
        third(d).start()
    for d in (0, 1):
        acc[d] = term(2 * SIGNS[d])
    for d in (0, 1):
        acc[5 + d] = term(SIGNS[d])
        near(d).start()
    mine = term(0)
    for d in (0, 1):
        third(d).wait_recv()
        acc[d] = acc[d] + third_buf[d]
        fourth(d).wait_recv()
        here = pl.ds(d * half_rows, half_rows)
        acc[d, here, :] = acc[d, here, :] + fourth_buf[d]
        relay(d).start()
    for d in (0, 1):
        near(d).wait_recv()
        mine = mine + near_buf[d]
    for d in (0, 1):
        relay(d).wait_recv()
        mine = mine + relay_buf[d]
    out[...] = mine
    for off in order:
        give(off).wait_send()
    for d in (0, 1):
        fourth(d).wait_send()
        third(d).wait_send()
        relay(d).wait_send()
        near(d).wait_send()


def z_scatter(part, nz):
    sem = pltpu.SemaphoreType.DMA
    return pl.pallas_call(
        functools.partial(z_scatter_kernel, nz),
        out_shape=jax.ShapeDtypeStruct((T, T), F32),
        in_specs=[VMEM],
        out_specs=VMEM,
        scratch_shapes=[
            pltpu.VMEM((nz, T, T), F32),
            pltpu.VMEM((7, T, T), F32),
            pltpu.VMEM((2, T, T), F32),
            pltpu.VMEM((2, T, T), F32),
            pltpu.VMEM((2, T, T), F32),
            pltpu.VMEM((2, T // 2, T), F32),
            sem((nz,)), sem((nz,)),
            sem((2, 4)), sem((2, 4)),
        ],
        compiler_params=pltpu.CompilerParams(collective_id=2, has_side_effects=True, vmem_limit_bytes=6 * MIB),
        name="z_scatter",
    )(part.reshape(nz, 2, T, T))


def local(nrow, ncol, features, weight, adj_tiles, tile_row, tile_col, slot_count, cotangent):
    nz, nx = nrow // 2, NX
    ny = ncol // nx
    rows, cols, count, adj = tile_row[0, 0], tile_col[0, 0], slot_count[0], adj_tiles[0, 0]
    in_hbm = [pltpu.with_memory_space_constraint(a, pltpu.HBM) for a in (features, adj, rows, cols)]
    x, adj, rows, cols = z_gather(*in_hbm, nz)
    partial = forward(rows, cols, count, adj, x.reshape(nrow, T, T), ny, nx)
    hidden, pre_rows, grad_weight = xy(partial, weight, cotangent, ny, nx, nrow)
    part, hidden, grad_weight = backward(rows, cols, count, adj, pre_rows, hidden, grad_weight, nrow, ny, nx)
    return hidden, z_scatter(part, nz).T, grad_weight


def solution(mesh):
    placed = (
        P(("col", "row"), None),
        P(),
        P("row", "col", None, None, None),
        P("row", "col", None),
        P("row", "col", None),
        P("row", "col"),
        P(("row", "col"), None),
    )
    return jax.shard_map(
        functools.partial(local, mesh.shape["row"], mesh.shape["col"]),
        mesh=mesh,
        in_specs=placed,
        out_specs=(P(("row", "col"), None), P(("col", "row"), None), P()),
        check_vma=False,
    )
```
